32 devices in a mesh: ctx: 8 (over y, x, core), tp: 4 (over z).
Axes of the slice: x: 2, y: 2, z: 4, core: 2. Of those that a mesh axis runs over, the one named last changes fastest.
Arguments:
- queries: bfloat16 [2048, 4096], P('ctx', 'tp'), may hold values from -6 to 6
- keys: bfloat16 [2048, 512], P('ctx'), may hold values from -6 to 6
- values: bfloat16 [2048, 512], P('ctx'), may hold values from -6 to 6
- out_weight: bfloat16 [4096, 8192], P('tp'), may hold values from -0.125 to 0.125
- storm_mask: int32 [16, 16], replicated, may hold values from 0 to 1, as said below
Outputs:
- mixed: bfloat16 [2048, 8192], P('ctx', 'tp')
The draws below stay inside these ranges and needn't reach their ends.
Inputs may be any that keep to these rules, and one draw needn't show every extreme that they name: storm_mask[i, j] is 0 where j > i and 1 where 0 <= i - j < 4.
All inputs are finite; a program needn't handle non-finite values.
Results may differ from the reference program's by a relative error of at most 0.019.
Values may be sent and summed in bfloat16 or wider, within the bound.
No kernel may reach another device: no remote copies, remote signals or barrier semaphores. Data moves between devices by JAX's collectives and lax.ppermute only.
A program may use at most 64 MiB of HBM per device.

```python
import jax
import jax.numpy as jnp
from jax import lax

D = 8192
HEADS = 32
KV_HEADS = 4
HDIM = 128
BLOCK = 128
BAND = 4
SEQUENCE_TOKENS = 2048
NB = 16
HD = 4096
GQ = 8
KEY_VALUE_WIDTH = 512
N_TP = 4


def paired_draw(key):
    width = HEADS * HDIM
    narrow = KV_HEADS * HDIM
    first_key, second_key = jax.random.split(jax.random.fold_in(key, 11), 2)
    query = jnp.clip(jax.random.normal(first_key, (SEQUENCE_TOKENS, width), jnp.float32), -6.0, 6.0)
    keyed = jnp.clip(jax.random.normal(second_key, (SEQUENCE_TOKENS, narrow), jnp.float32), -6.0, 6.0)
    return (query, keyed)


def draw_queries(key, part):
    return paired_draw(key)[0].astype(jnp.bfloat16)


def draw_keys(key, part):
    return paired_draw(key)[1].astype(jnp.bfloat16)


def draw_storm_mask(key, part):
    coins = jax.random.randint(jax.random.fold_in(key, 29), (NB, NB), 0, 4) == 0
    later = jnp.arange(NB)[:, None]
    earlier = jnp.arange(NB)[None, :]
    near = (earlier <= later) & (later - earlier < BAND)
    distant = (earlier < later) & coins
    return (near | distant).astype(jnp.int32)


def raised(drawn, rng, source, target, parts, factor):
    def block_of(dim):
        return (jnp.arange(drawn.shape[dim]) // (drawn.shape[dim] // parts)).reshape((-1,) + (1,) * (drawn.ndim - 1 - dim))

    one_side = jax.random.permutation(rng, parts)[block_of(target)]
    second = (block_of(target) + parts // 2) % parts
    return jnp.where((block_of(source) == one_side) | (block_of(source) == second), factor * drawn, drawn)


def steps_of(rng, dims, shards, low, high):
    def one(axis_at, parts):
        heights = jax.random.uniform(jax.random.fold_in(jax.random.fold_in(rng, 6), axis_at), (parts,), jnp.float32, low / len(shards), high / len(shards))
        return jnp.repeat(jnp.exp(heights), dims[axis_at] // parts).reshape((-1,) + (1,) * (len(dims) - axis_at - 1))

    gain = one(*shards[0])
    for cut in shards[1:]:
        gain = gain * one(*cut)
    return gain


def noise(stream_key, shape, scale, limit, cuts=(), held_as=jnp.bfloat16):
    factor_of = steps_of(stream_key, shape, cuts, -0.22, 0.18) if cuts else 1.0
    result = jax.random.normal(stream_key, shape, jnp.float32) * scale * factor_of
    return jnp.minimum(jnp.maximum(result, -limit), limit).astype(held_as)


def heavy_noise(rng, extent, scale, bound, pieces, heavy, held_as=jnp.bfloat16):
    values = scale * jax.random.normal(rng, extent, jnp.float32)
    if pieces:
        values = values * steps_of(rng, extent, pieces, -0.22, 0.18)
    return jnp.clip(raised(values, jax.random.fold_in(rng, 3), *heavy), -bound, bound).astype(held_as)


def setup_inputs(seed: int = 0) -> dict:
    streams_of = jax.random.split(jax.random.key(seed), 6)
    queries = draw_queries(jax.random.fold_in(streams_of[5], 71), 0)
    keys = draw_keys(jax.random.fold_in(streams_of[5], 71), 0)
    values = noise(streams_of[2], (SEQUENCE_TOKENS, KEY_VALUE_WIDTH), 1.0, 6.0, ((0, 8),))
    out_weight = heavy_noise(streams_of[3], (HD, D), HD ** -0.5, 0.125, ((0, 4),), (0, 1, 4, 2.0))
    storm_mask = draw_storm_mask(jax.random.fold_in(streams_of[5], 71), 0)
    return {"queries": queries, "keys": keys, "values": values, "out_weight": out_weight, "storm_mask": storm_mask}


def reference(queries, keys, values, out_weight, storm_mask):
    length = queries.shape[0]
    scale = HDIM ** -0.5
    block_of = jnp.arange(length) // BLOCK
    allowed = storm_mask[block_of][:, block_of] == 1

    def heads_first(array, count):
        return array.reshape(length, count, HDIM).transpose(1, 0, 2)

    def one_head(operands):
        query, keyed, weighted_values = operands
        scores = jnp.dot(query, keyed.T, preferred_element_type=jnp.float32) * scale
        scores = jnp.where(allowed, scores, -1e30)
        peak = jnp.max(scores, axis=1, keepdims=True)
        weights = jnp.where(allowed, jnp.exp(scores - peak), 0.0)
        total = jnp.sum(weights, axis=1, keepdims=True)
        summed = jnp.dot(weights.astype(jnp.bfloat16), weighted_values, preferred_element_type=jnp.float32)
        return (summed / total).astype(jnp.bfloat16)

    keyed_all = jnp.repeat(heads_first(keys, KV_HEADS), GQ, axis=0)
    valued_all = jnp.repeat(heads_first(values, KV_HEADS), GQ, axis=0)
    attended = lax.map(one_head, (heads_first(queries, HEADS), keyed_all, valued_all))
    attended = attended.transpose(1, 0, 2).reshape(length, HEADS * HDIM)
    group = HEADS * HDIM // N_TP
    output_rows = jnp.zeros((length, D), jnp.float32)
    for number in range(N_TP):
        partial_value = jnp.dot(attended[:, number * group:(number + 1) * group], out_weight[number * group:(number + 1) * group], preferred_element_type=jnp.float32).astype(jnp.bfloat16)
        output_rows = output_rows + lax.optimization_barrier(partial_value).astype(jnp.float32)
    return output_rows.astype(jnp.bfloat16)
```

```python
import functools
import math

import jax
import jax.numpy as jnp
from jax import lax
from jax.experimental import pallas as pl
from jax.experimental.pallas import tpu as pltpu
from jax.sharding import PartitionSpec as P

HDIM = 128
BLOCK = 128
GQ = 8
TILE = 512
EXPONENT = HDIM ** (-0.5) * math.log2(math.e)
VMEM_LIMIT = 48 * 1024 * 1024


def pack_kernel(head_ref, keys_ref, values_ref, out_ref):
    out_ref[:, :HDIM] = keys_ref[...]
    out_ref[:, HDIM:] = values_ref[...]


def pack_head(keys, values, head):
    rows = keys.shape[0]
    block = pl.BlockSpec((rows, HDIM), lambda i, head: (0, head[0]))
    return pl.pallas_call(
        pack_kernel,
        grid_spec=pltpu.PrefetchScalarGridSpec(
            num_scalar_prefetch=1,
            grid=(1,),
            in_specs=[block, block],
            out_specs=pl.BlockSpec((rows, 2 * HDIM), lambda i, head: (0, 0)),
        ),
        out_shape=jax.ShapeDtypeStruct((rows, 2 * HDIM), keys.dtype),
        name="pack_head",
    )(head.reshape(1), keys, values)


def attention_kernel(parts, owners_ref, mask_ref, query_ref, *refs):
    kv_refs = refs[:parts]
    out_ref, kv, scores, peak, total, summed, chosen = refs[parts:]
    rows, width = query_ref.shape
    heads = width // HDIM
    per_device = rows // BLOCK
    place = owners_ref[kv.shape[0]]
    at = 0
    for ref in kv_refs:
        count = ref.shape[0]
        kv[at : at + count] = ref[...]
        at += count
    owners = at

    for block in range(per_device):
        row = place * per_device + block
        top = slice(block * BLOCK, (block + 1) * BLOCK)

        def choose(slot, found):
            for part in range(per_device):
                here = mask_ref[row, owners_ref[slot] * per_device + part] == 1
                chosen[found] = slot * per_device + part
                found = found + here.astype(jnp.int32)
            return found

        found = lax.fori_loop(0, owners, choose, jnp.int32(0))
        pairs = (found + 1) // 2

        @pl.when(found % 2 == 1)
        def _():
            chosen[found] = chosen[found - 1]

        def tile(number):
            index = chosen[number]
            slot = index // per_device
            first = pl.multiple_of((index % per_device) * BLOCK, BLOCK)
            return slot, pl.ds(first, BLOCK)

        peak[...] = jnp.full(peak.shape, -1e30, jnp.float32)
        total[...] = jnp.zeros(total.shape, jnp.float32)
        summed[...] = jnp.zeros(summed.shape, jnp.float32)

        def score(pair, carry):
            slot0, rows0 = tile(2 * pair)
            slot1, rows1 = tile(2 * pair + 1)
            keys = jnp.concatenate([kv[slot0, rows0, :HDIM], kv[slot1, rows1, :HDIM]], axis=0)
            for head in range(heads):
                query = query_ref[top, head * HDIM : (head + 1) * HDIM]
                found_scores = lax.dot_general(
                    query, keys, (((1,), (1,)), ((), ())), preferred_element_type=jnp.float32
                )
                scores[pair, head] = found_scores
                peak[head] = jnp.maximum(
                    peak[head], jnp.maximum(found_scores[:, :BLOCK], found_scores[:, BLOCK:])
                )
            return carry

        lax.fori_loop(0, pairs, score, 0)

        @pl.when(found % 2 == 1)
        def _():
            scores[pairs - 1, :, :, BLOCK:] = jnp.full((heads, BLOCK, BLOCK), -1e30, jnp.float32)

        for head in range(heads):
            peak[head] = jnp.broadcast_to(
                jnp.max(peak[head], axis=1, keepdims=True), (BLOCK, BLOCK)
            )

        def weigh(pair, carry):
            slot0, rows0 = tile(2 * pair)
            slot1, rows1 = tile(2 * pair + 1)
            values = jnp.concatenate([kv[slot0, rows0, HDIM:], kv[slot1, rows1, HDIM:]], axis=0)
            for head in range(heads):
                highest = peak[head]
                left = jnp.exp2((scores[pair, head, :, :BLOCK] - highest) * EXPONENT)
                right = jnp.exp2((scores[pair, head, :, BLOCK:] - highest) * EXPONENT)
                total[head] += left + right
                weights = jnp.concatenate([left, right], axis=1).astype(jnp.bfloat16)
                summed[head] += jnp.dot(weights, values, preferred_element_type=jnp.float32)
            return carry

        lax.fori_loop(0, pairs, weigh, 0)

        for head in range(heads):
            norm = jnp.sum(total[head], axis=1, keepdims=True)
            out_ref[top, head * HDIM : (head + 1) * HDIM] = (summed[head] / norm).astype(
                jnp.bfloat16
            )


def attend(query, kv_parts, owners, place, storm_mask):
    rows, width = query.shape
    heads = width // HDIM
    count = owners.shape[0]
    blocks = count * (rows // BLOCK)
    return pl.pallas_call(
        functools.partial(attention_kernel, len(kv_parts)),
        in_specs=[pl.BlockSpec(memory_space=pltpu.SMEM)] * 2
        + [pl.BlockSpec(memory_space=pltpu.VMEM)] * (1 + len(kv_parts)),
        out_specs=pl.BlockSpec(memory_space=pltpu.VMEM),
        out_shape=jax.ShapeDtypeStruct((rows, width), jnp.bfloat16),
        scratch_shapes=[
            pltpu.VMEM((count, rows, 2 * HDIM), jnp.bfloat16),
            pltpu.VMEM(((blocks + 1) // 2, heads, BLOCK, 2 * BLOCK), jnp.float32),
            pltpu.VMEM((heads, BLOCK, BLOCK), jnp.float32),
            pltpu.VMEM((heads, BLOCK, BLOCK), jnp.float32),
            pltpu.VMEM((heads, BLOCK, HDIM), jnp.float32),
            pltpu.SMEM((blocks + 2,), jnp.int32),
        ],
        compiler_params=pltpu.CompilerParams(vmem_limit_bytes=VMEM_LIMIT),
        name="attend",
    )(jnp.append(owners, place).astype(jnp.int32), storm_mask, query, *kv_parts)


def project_kernel(first_ref, attended_ref, weight_ref, out_ref):
    out_ref[...] = jnp.dot(
        attended_ref[...], weight_ref[...], preferred_element_type=jnp.float32
    ).astype(jnp.bfloat16)


def project(attended, out_weight, first, columns):
    rows, depth = attended.shape
    tile = min(TILE, columns)
    return pl.pallas_call(
        project_kernel,
        grid_spec=pltpu.PrefetchScalarGridSpec(
            num_scalar_prefetch=1,
            grid=(columns // tile,),
            in_specs=[
                pl.BlockSpec((rows, depth), lambda i, first: (0, 0)),
                pl.BlockSpec((depth, tile), lambda i, first: (0, first[0] + i)),
            ],
            out_specs=pl.BlockSpec((rows, tile), lambda i, first: (0, i)),
        ),
        out_shape=jax.ShapeDtypeStruct((rows, columns), jnp.bfloat16),
        compiler_params=pltpu.CompilerParams(vmem_limit_bytes=VMEM_LIMIT),
        name="project",
    )((first // tile).astype(jnp.int32).reshape(1), attended, out_weight)


def gather_heads(packed, place, devices):
    if devices != 8:
        everyone = lax.all_gather(packed, "ctx", axis=0, tiled=False)
        order = jnp.arange(devices, dtype=jnp.int32)
        return [everyone], order
    packed = packed[None]

    def swap(array, bits):
        return lax.ppermute(array, "ctx", [(i, i ^ bits) for i in range(devices)])

    near = [packed] + [swap(packed, bits) for bits in (6, 2, 4)]
    other = [swap(array, 1) for array in near]
    order = place ^ jnp.array([0, 6, 2, 4, 1, 7, 3, 5], jnp.int32)
    return near + other, order


def added(*arrays):
    wide = [array.astype(jnp.float32) for array in arrays]
    return functools.reduce(lambda a, b: a + b, wide).astype(jnp.bfloat16)


def line_sum(attended, out_weight):
    place = lax.axis_index("tp")
    quarter = out_weight.shape[1] // 4
    upper = place >= 2
    outer = (place == 0) | (place == 3)
    far_outer = jnp.where(upper, 0, 3) * quarter
    far_inner = jnp.where(upper, 1, 2) * quarter
    near = jnp.where(upper, 5 - place, 1 - place) * quarter
    own = place * quarter

    def inward(array):
        return lax.ppermute(array, "tp", [(0, 1), (3, 2)])

    def across(array):
        return lax.ppermute(array, "tp", [(1, 2), (2, 1)])

    def outward(array):
        return lax.ppermute(array, "tp", [(1, 0), (2, 3)])

    def chunks(first, sizes):
        at = 0
        for size in sizes:
            yield project(attended, out_weight, first + at, size)
            at += size

    half = quarter // 2
    fourth = quarter // 4
    to_outer = []
    for partial in chunks(far_outer, (fourth, fourth, half)):
        to_outer.append(across(added(partial, inward(partial))))
    to_own = []
    for partial in chunks(far_inner, (half, half)):
        to_own.append(across(added(partial, inward(partial))))
    nearby = list(chunks(near, (fourth, fourth, half)))
    direct = [inward(partial) for partial in nearby]
    returned = [outward(added(partial, far)) for partial, far in zip(nearby, to_outer)]
    mine = project(attended, out_weight, own, quarter)
    return added(
        mine,
        jnp.concatenate(direct, axis=1),
        jnp.concatenate(to_own, axis=1),
        jnp.concatenate(returned, axis=1),
    )


def body(mesh, queries, keys, values, out_weight, storm_mask):
    place = lax.axis_index("ctx")
    heads = queries.shape[1] // HDIM
    shared_head = lax.axis_index("tp") * heads // GQ
    packed = pack_head(keys, values, shared_head)
    kv_parts, order = gather_heads(packed, place, mesh.shape["ctx"])
    attended = attend(queries, kv_parts, order, place, storm_mask)
    if mesh.shape["tp"] == 4:
        return line_sum(attended, out_weight)
    partial = project(attended, out_weight, jnp.int32(0), out_weight.shape[1])
    return lax.psum_scatter(partial, "tp", scatter_dimension=1, tiled=True)


def solution(mesh):
    placed = (P("ctx", "tp"), P("ctx", None), P("ctx", None), P("tp", None), P())
    return jax.shard_map(
        functools.partial(body, mesh),
        mesh=mesh,
        in_specs=placed,
        out_specs=P("ctx", "tp"),
        check_vma=False,
    )
```

```python
import functools
import math

import jax
import jax.numpy as jnp
from jax import lax
from jax.experimental import pallas as pl
from jax.experimental.pallas import tpu as pltpu
from jax.sharding import PartitionSpec as P

HDIM = 128
BLOCK = 128
GQ = 8
TILE = 512
EXPONENT = HDIM ** (-0.5) * math.log2(math.e)
VMEM_LIMIT = 48 * 1024 * 1024


def pack_kernel(head_ref, keys_ref, values_ref, out_ref):
    out_ref[:, :HDIM] = keys_ref[...]
    out_ref[:, HDIM:] = values_ref[...]


def pack_head(keys, values, head):
    rows = keys.shape[0]
    block = pl.BlockSpec((rows, HDIM), lambda i, head: (0, head[0]))
    return pl.pallas_call(
        pack_kernel,
        grid_spec=pltpu.PrefetchScalarGridSpec(
            num_scalar_prefetch=1,
            grid=(1,),
            in_specs=[block, block],
            out_specs=pl.BlockSpec((rows, 2 * HDIM), lambda i, head: (0, 0)),
        ),
        out_shape=jax.ShapeDtypeStruct((rows, 2 * HDIM), keys.dtype),
        name="pack_head",
    )(head.reshape(1), keys, values)


def attention_kernel(parts, swaps, place_ref, mask_ref, query_hbm, own_hbm, *refs):
    kv_refs = refs[:parts]
    out_ref, query_ref, kv, scores, peak, total, summed, chosen, arrived = refs[parts:]
    rows, width = query_ref.shape
    heads = width // HDIM
    per_device = rows // BLOCK
    place = place_ref[0]
    owners = kv.shape[0]
    loads = [pltpu.make_async_copy(query_hbm, query_ref, arrived.at[0])]
    if swaps:
        loads.append(pltpu.make_async_copy(own_hbm, kv.at[0], arrived.at[1]))
    for load in loads:
        load.start()
    at = len(loads) - 1
    for ref in kv_refs:
        count = ref.shape[0]
        kv[at : at + count] = ref[...]
        at += count
    for load in loads:
        load.wait()

    for block in range(per_device):
        row = place * per_device + block
        top = slice(block * BLOCK, (block + 1) * BLOCK)

        def choose(slot, found):
            owner = place ^ swaps[slot] if swaps else slot
            for part in range(per_device):
                here = mask_ref[row, owner * per_device + part] == 1
                chosen[found] = slot * per_device + part
                found = found + here.astype(jnp.int32)
            return found

        found = jnp.int32(0)
        if swaps:
            for slot in range(owners):
                found = choose(slot, found)
        else:
            found = lax.fori_loop(0, owners, choose, found)
        pairs = (found + 1) // 2

        @pl.when(found % 2 == 1)
        def _():
            chosen[found] = chosen[found - 1]

        def tile(number):
            index = chosen[number]
            slot = index // per_device
            first = pl.multiple_of((index % per_device) * BLOCK, BLOCK)
            return slot, pl.ds(first, BLOCK)

        peak[...] = jnp.full(peak.shape, -1e30, jnp.float32)
        total[...] = jnp.zeros(total.shape, jnp.float32)
        summed[...] = jnp.zeros(summed.shape, jnp.float32)

        def score(pair, carry):
            slot0, rows0 = tile(2 * pair)
            slot1, rows1 = tile(2 * pair + 1)
            keys = jnp.concatenate([kv[slot0, rows0, :HDIM], kv[slot1, rows1, :HDIM]], axis=0)
            for head in range(heads):
                query = query_ref[top, head * HDIM : (head + 1) * HDIM]
                found_scores = lax.dot_general(
                    query, keys, (((1,), (1,)), ((), ())), preferred_element_type=jnp.float32
                )
                scores[pair, head] = found_scores
                peak[head] = jnp.maximum(
                    peak[head], jnp.maximum(found_scores[:, :BLOCK], found_scores[:, BLOCK:])
                )
            return carry

        lax.fori_loop(0, pairs, score, 0)

        @pl.when(found % 2 == 1)
        def _():
            scores[pairs - 1, :, :, BLOCK:] = jnp.full((heads, BLOCK, BLOCK), -1e30, jnp.float32)

        for head in range(heads):
            peak[head] = jnp.broadcast_to(
                jnp.max(peak[head], axis=1, keepdims=True), (BLOCK, BLOCK)
            )

        def weigh(pair, carry):
            slot0, rows0 = tile(2 * pair)
            slot1, rows1 = tile(2 * pair + 1)
            values = jnp.concatenate([kv[slot0, rows0, HDIM:], kv[slot1, rows1, HDIM:]], axis=0)
            for head in range(heads):
                highest = peak[head]
                left = jnp.exp2((scores[pair, head, :, :BLOCK] - highest) * EXPONENT)
                right = jnp.exp2((scores[pair, head, :, BLOCK:] - highest) * EXPONENT)
                total[head] += left + right
                weights = jnp.concatenate([left, right], axis=1).astype(jnp.bfloat16)
                summed[head] += jnp.dot(weights, values, preferred_element_type=jnp.float32)
            return carry

        lax.fori_loop(0, pairs, weigh, 0)

        for head in range(heads):
            norm = jnp.sum(total[head], axis=1, keepdims=True)
            out_ref[top, head * HDIM : (head + 1) * HDIM] = (summed[head] / norm).astype(
                jnp.bfloat16
            )


def attend(query, own, others, swaps, place, storm_mask):
    rows, width = query.shape
    heads = width // HDIM
    count = len(swaps) if swaps else others[0].shape[0]
    blocks = count * (rows // BLOCK)
    return pl.pallas_call(
        functools.partial(attention_kernel, len(others), swaps),
        grid_spec=pltpu.PrefetchScalarGridSpec(
            num_scalar_prefetch=2,
            grid=(1,),
            in_specs=[pl.BlockSpec(memory_space=pltpu.HBM)] * 2
            + [pl.BlockSpec(memory_space=pltpu.VMEM)] * len(others),
            out_specs=pl.BlockSpec(memory_space=pltpu.VMEM),
            scratch_shapes=[
                pltpu.VMEM((rows, width), jnp.bfloat16),
                pltpu.VMEM((count, rows, 2 * HDIM), jnp.bfloat16),
                pltpu.VMEM(((blocks + 1) // 2, heads, BLOCK, 2 * BLOCK), jnp.float32),
                pltpu.VMEM((heads, BLOCK, BLOCK), jnp.float32),
                pltpu.VMEM((heads, BLOCK, BLOCK), jnp.float32),
                pltpu.VMEM((heads, BLOCK, HDIM), jnp.float32),
                pltpu.SMEM((blocks + 2,), jnp.int32),
                pltpu.SemaphoreType.DMA((2,)),
            ],
        ),
        out_shape=jax.ShapeDtypeStruct((rows, width), jnp.bfloat16),
        compiler_params=pltpu.CompilerParams(vmem_limit_bytes=VMEM_LIMIT),
        name="attend",
    )(place.astype(jnp.int32).reshape(1), storm_mask, query, own, *others)


def project_kernel(first_ref, attended_ref, weight_ref, out_ref):
    out_ref[...] = jnp.dot(
        attended_ref[...], weight_ref[...], preferred_element_type=jnp.float32
    ).astype(jnp.bfloat16)


def project(attended, out_weight, first, columns):
    rows, depth = attended.shape
    tile = min(TILE, columns)
    return pl.pallas_call(
        project_kernel,
        grid_spec=pltpu.PrefetchScalarGridSpec(
            num_scalar_prefetch=1,
            grid=(columns // tile,),
            in_specs=[
                pl.BlockSpec((rows, depth), lambda i, first: (0, 0)),
                pl.BlockSpec((depth, tile), lambda i, first: (0, first[0] + i)),
            ],
            out_specs=pl.BlockSpec((rows, tile), lambda i, first: (0, i)),
        ),
        out_shape=jax.ShapeDtypeStruct((rows, columns), jnp.bfloat16),
        compiler_params=pltpu.CompilerParams(vmem_limit_bytes=VMEM_LIMIT),
        name="project",
    )((first // tile).astype(jnp.int32).reshape(1), attended, out_weight)


def gather_heads(packed, devices):
    if devices != 8:
        return [lax.all_gather(packed, "ctx", axis=0, tiled=False)], ()

    def swap(array, bits):
        return lax.ppermute(array, "ctx", [(i, i ^ bits) for i in range(devices)])

    near = [packed[None]] + [swap(packed[None], bits) for bits in (6, 2, 4)]
    other = [swap(array, 1) for array in near]
    return near[1:] + other, (0, 6, 2, 4, 1, 7, 3, 5)


def after(array, *earlier):
    return lax.optimization_barrier((array, *earlier))[0]


def added(*arrays):
    wide = [array.astype(jnp.float32) for array in arrays]
    return functools.reduce(lambda a, b: a + b, wide).astype(jnp.bfloat16)


def line_sum(attended, out_weight):
    place = lax.axis_index("tp")
    quarter = out_weight.shape[1] // 4
    upper = place >= 2
    far_outer = jnp.where(upper, 0, 3) * quarter
    far_inner = jnp.where(upper, 1, 2) * quarter
    near = jnp.where(upper, 5 - place, 1 - place) * quarter
    own = place * quarter
    half = quarter // 2
    fourth = quarter // 4
    pieces = ((0, fourth), (fourth, fourth), (half, half))
    halves = ((0, half), (half, half))
    projected, chain = [], []

    def part(first, columns):
        source = after(attended, projected[-1]) if projected else attended
        projected.append(project(source, out_weight, first, columns))
        return projected[-1]

    def step(*arrays):
        first = after(arrays[0], chain[-1]) if chain else arrays[0]
        chain.append(added(first, *arrays[1:]))
        return chain[-1]

    def inward(array):
        return lax.ppermute(array, "tp", [(0, 1), (3, 2)])

    def across(array):
        return lax.ppermute(array, "tp", [(1, 2), (2, 1)])

    def outward(array):
        return lax.ppermute(array, "tp", [(1, 0), (2, 3)])

    outer_parts = [part(far_outer + at, size) for at, size in pieces]
    outer_sums = [inward(array) for array in outer_parts]
    inner_parts = [part(far_inner + at, size) for at, size in halves]
    inner_sums = [inward(array) for array in inner_parts]
    near_parts = [part(near + at, size) for at, size in halves]
    direct = [inward(array) for array in near_parts]
    mine = part(own, quarter)
    near_pieces = [near_parts[0][:, :fourth], near_parts[0][:, fourth:], near_parts[1]]

    to_outer, to_own, returned = [None] * 3, [None] * 2, [None] * 3
    for kind, at in (("f", 0), ("f", 1), ("o", 0), ("o", 1), ("f", 2), ("n", 0), ("o", 2), ("n", 1)):
        if kind == "f":
            to_outer[at] = across(step(outer_parts[at], outer_sums[at]))
        elif kind == "o":
            returned[at] = outward(step(near_pieces[at], to_outer[at]))
        else:
            to_own[at] = across(step(inner_parts[at], inner_sums[at]))
    left = step(mine[:, :half], jnp.concatenate(returned[:2], axis=1), to_own[0], direct[0])
    right = step(mine[:, half:], returned[2], to_own[1], direct[1])
    return jnp.concatenate([left, right], axis=1)


def body(mesh, queries, keys, values, out_weight, storm_mask):
    place = lax.axis_index("ctx")
    heads = queries.shape[1] // HDIM
    shared_head = lax.axis_index("tp") * heads // GQ
    packed = pack_head(keys, values, shared_head)
    others, swaps = gather_heads(packed, mesh.shape["ctx"])
    attended = attend(queries, packed, others, swaps, place, storm_mask)
    if mesh.shape["tp"] == 4:
        return line_sum(attended, out_weight)
    partial = project(attended, out_weight, jnp.int32(0), out_weight.shape[1])
    return lax.psum_scatter(partial, "tp", scatter_dimension=1, tiled=True)


def solution(mesh):
    placed = (P("ctx", "tp"), P("ctx", None), P("ctx", None), P("tp", None), P())
    return jax.shard_map(
        functools.partial(body, mesh),
        mesh=mesh,
        in_specs=placed,
        out_specs=P("ctx", "tp"),
        check_vma=False,
    )
```

```python
import functools
import math

import jax
import jax.numpy as jnp
from jax import lax
from jax.experimental import pallas as pl
from jax.experimental.pallas import tpu as pltpu
from jax.sharding import PartitionSpec as P

HDIM = 128
BLOCK = 128
GQ = 8
TILE = 512
EXPONENT = HDIM ** (-0.5) * math.log2(math.e)
VMEM_LIMIT = 48 * 1024 * 1024


def pack_head(keys, values, head):
    return jnp.concatenate(
        [lax.dynamic_slice_in_dim(array, head * HDIM, HDIM, 1) for array in (keys, values)], axis=1
    )


def choose_blocks(place, swaps, owners, row, per_device, mask_ref, chosen):
    def choose(slot, found):
        owner = place ^ swaps[slot] if swaps else slot
        for part in range(per_device):
            here = mask_ref[row, owner * per_device + part] == 1
            chosen[found] = slot * per_device + part
            found = found + here.astype(jnp.int32)
        return found

    found = jnp.int32(0)
    if swaps:
        for slot in range(owners):
            found = choose(slot, found)
    else:
        found = lax.fori_loop(0, owners, choose, found)

    @pl.when(found % 2 == 1)
    def _():
        chosen[found] = chosen[found - 1]

    return found


def attention_kernel(parts, swaps, first, place_ref, mask_ref, query_ref, *refs):
    if first:
        own_hbm, *refs = refs
        kv_refs = refs[:parts]
        query_out, peaks_out, totals_out, sums_out, kv, scores, peak, chosen, arrived = refs[parts:]
        loads = [pltpu.make_async_copy(query_ref, query_out, arrived.at[0])]
        if swaps:
            loads.append(pltpu.make_async_copy(own_hbm, kv.at[0], arrived.at[1]))
        for load in loads:
            load.start()
        at = len(loads) - 1
    else:
        peaks_in, totals_in, sums_in, *refs = refs
        kv_refs = refs[:parts]
        out_ref, kv, scores, peak, total, summed, chosen = refs[parts:]
        at = 0
    for ref in kv_refs:
        count = ref.shape[0]
        kv[at : at + count] = ref[...]
        at += count
    if first:
        for load in loads:
            load.wait()
        query_ref = query_out
    rows, width = query_ref.shape
    heads = width // HDIM
    per_device = rows // BLOCK
    place = place_ref[0]
    owners = kv.shape[0]

    for block in range(per_device):
        top = slice(block * BLOCK, (block + 1) * BLOCK)
        found = choose_blocks(
            place, swaps, owners, place * per_device + block, per_device, mask_ref, chosen
        )
        pairs = (found + 1) // 2

        def tile(number):
            index = chosen[number]
            start = pl.multiple_of((index % per_device) * BLOCK, BLOCK)
            return index // per_device, pl.ds(start, BLOCK)

        if first:
            total, summed = totals_out.at[block], sums_out.at[block]
            peak[...] = jnp.full(peak.shape, -1e30, jnp.float32)
            total[...] = jnp.zeros(total.shape, jnp.float32)
            summed[...] = jnp.zeros(summed.shape, jnp.float32)
        else:
            peak[...] = peaks_in[block]

        def score(pair, carry):
            slot0, rows0 = tile(2 * pair)
            slot1, rows1 = tile(2 * pair + 1)
            keys = jnp.concatenate([kv[slot0, rows0, :HDIM], kv[slot1, rows1, :HDIM]], axis=0)
            for head in range(heads):
                query = query_ref[top, head * HDIM : (head + 1) * HDIM]
                here = lax.dot_general(
                    query, keys, (((1,), (1,)), ((), ())), preferred_element_type=jnp.float32
                )
                scores[pair, head] = here
                peak[head] = jnp.maximum(
                    peak[head], jnp.maximum(here[:, :BLOCK], here[:, BLOCK:])
                )
            return carry

        lax.fori_loop(0, pairs, score, 0)

        @pl.when(found % 2 == 1)
        def _():
            scores[pairs - 1, :, :, BLOCK:] = jnp.full((heads, BLOCK, BLOCK), -1e30, jnp.float32)

        for head in range(heads):
            highest = jnp.max(peak[head], axis=1, keepdims=True)
            peak[head] = jnp.broadcast_to(highest, (BLOCK, BLOCK))
            if not first:
                factor = jnp.exp2((peaks_in[block, head] - peak[head]) * EXPONENT)
                total[head] = totals_in[block, head] * factor
                summed[head] = sums_in[block, head] * factor

        def weigh(pair, carry):
            slot0, rows0 = tile(2 * pair)
            slot1, rows1 = tile(2 * pair + 1)
            values = jnp.concatenate([kv[slot0, rows0, HDIM:], kv[slot1, rows1, HDIM:]], axis=0)
            for head in range(heads):
                highest = peak[head]
                left = jnp.exp2((scores[pair, head, :, :BLOCK] - highest) * EXPONENT)
                right = jnp.exp2((scores[pair, head, :, BLOCK:] - highest) * EXPONENT)
                total[head] += left + right
                weights = jnp.concatenate([left, right], axis=1).astype(jnp.bfloat16)
                summed[head] += jnp.dot(weights, values, preferred_element_type=jnp.float32)
            return carry

        lax.fori_loop(0, pairs, weigh, 0)

        if first:
            peaks_out[block] = peak[...]
        else:
            for head in range(heads):
                norm = jnp.sum(total[head], axis=1, keepdims=True)
                out_ref[top, head * HDIM : (head + 1) * HDIM] = (summed[head] / norm).astype(
                    jnp.bfloat16
                )


def attention_part(first, swaps, count, place, storm_mask, query, state, parts):
    rows, width = query.shape
    heads = width // HDIM
    blocks = count * (rows // BLOCK)
    vmem = pl.BlockSpec(memory_space=pltpu.VMEM)
    hbm = pl.BlockSpec(memory_space=pl.ANY)
    running = (rows // BLOCK, heads, BLOCK, BLOCK)
    taken = jax.ShapeDtypeStruct((rows, width), jnp.bfloat16)
    scratch = [
        pltpu.VMEM((count, rows, 2 * HDIM), jnp.bfloat16),
        pltpu.VMEM(((blocks + 1) // 2, heads, BLOCK, 2 * BLOCK), jnp.float32),
        pltpu.VMEM((heads, BLOCK, BLOCK), jnp.float32),
    ]
    if first:
        specs = [hbm, hbm] + [vmem] * len(parts)
        out_shape = [taken] + [jax.ShapeDtypeStruct(running, jnp.float32)] * 3
    else:
        specs = [vmem] * (4 + len(parts))
        out_shape = taken
        scratch += [pltpu.VMEM((heads, BLOCK, BLOCK), jnp.float32)] * 2
    scratch += [pltpu.SMEM((blocks + 2,), jnp.int32)]
    if first:
        scratch += [pltpu.SemaphoreType.DMA((2,))]
    return pl.pallas_call(
        functools.partial(attention_kernel, len(parts), swaps, first),
        grid_spec=pltpu.PrefetchScalarGridSpec(
            num_scalar_prefetch=2,
            grid=(1,),
            in_specs=specs,
            out_specs=[vmem] * 4 if first else vmem,
            scratch_shapes=scratch,
        ),
        out_shape=out_shape,
        compiler_params=pltpu.CompilerParams(vmem_limit_bytes=VMEM_LIMIT),
        name="attend_first" if first else "attend_rest",
    )(place.astype(jnp.int32).reshape(1), storm_mask, query, *state, *parts)


def attend(queries, packed, place, devices, storm_mask):
    if devices != 8:
        everyone = lax.all_gather(packed, "ctx", axis=0, tiled=False)
        state = attention_part(
            True, (), devices, place, storm_mask, queries, [packed], [everyone]
        )
        query, *state = state
        nothing = jnp.zeros_like(storm_mask)
        return attention_part(
            False, (), 1, place, nothing, query, state, [everyone[:1]]
        )

    def swap(array, bits):
        return lax.ppermute(array, "ctx", [(i, i ^ bits) for i in range(devices)])

    near = [swap(packed[None], bits) for bits in (6, 2, 4)]
    query, *state = attention_part(
        True, (0, 1), 2, place, storm_mask, queries, [packed], [swap(packed[None], 1)]
    )
    other = [swap(array, 1) for array in near]
    return attention_part(
        False, (6, 2, 4, 7, 3, 5), 6, place, storm_mask, query, state, near + other
    )


def project_kernel(first_ref, attended_ref, weight_ref, out_ref):
    out_ref[...] = jnp.dot(
        attended_ref[...], weight_ref[...], preferred_element_type=jnp.float32
    ).astype(jnp.bfloat16)


def project(attended, out_weight, first, columns):
    rows, depth = attended.shape
    tile = min(TILE, columns)
    return pl.pallas_call(
        project_kernel,
        grid_spec=pltpu.PrefetchScalarGridSpec(
            num_scalar_prefetch=1,
            grid=(columns // tile,),
            in_specs=[
                pl.BlockSpec((rows, depth), lambda i, first: (0, 0)),
                pl.BlockSpec((depth, tile), lambda i, first: (0, first[0] + i)),
            ],
            out_specs=pl.BlockSpec((rows, tile), lambda i, first: (0, i)),
        ),
        out_shape=jax.ShapeDtypeStruct((rows, columns), jnp.bfloat16),
        compiler_params=pltpu.CompilerParams(vmem_limit_bytes=VMEM_LIMIT),
        name="project",
    )((first // tile).astype(jnp.int32).reshape(1), attended, out_weight)


def after(array, *earlier):
    return lax.optimization_barrier((array, *earlier))[0]


def added(*arrays):
    wide = [array.astype(jnp.float32) for array in arrays]
    return functools.reduce(lambda a, b: a + b, wide).astype(jnp.bfloat16)


def line_sum(attended, out_weight):
    place = lax.axis_index("tp")
    quarter = out_weight.shape[1] // 4
    upper = place >= 2
    far_outer = jnp.where(upper, 0, 3) * quarter
    far_inner = jnp.where(upper, 1, 2) * quarter
    near = jnp.where(upper, 5 - place, 1 - place) * quarter
    own = place * quarter
    half = quarter // 2
    fourth = quarter // 4
    pieces = ((0, fourth), (fourth, fourth), (half, half))
    halves = ((0, half), (half, half))
    projected, chain = [], []

    def part(first, columns):
        source = after(attended, projected[-1]) if projected else attended
        projected.append(project(source, out_weight, first, columns))
        return projected[-1]

    def step(*arrays):
        first = after(arrays[0], chain[-1]) if chain else arrays[0]
        chain.append(added(first, *arrays[1:]))
        return chain[-1]

    def inward(array):
        return lax.ppermute(array, "tp", [(0, 1), (3, 2)])

    def across(array):
        return lax.ppermute(array, "tp", [(1, 2), (2, 1)])

    def outward(array):
        return lax.ppermute(array, "tp", [(1, 0), (2, 3)])

    outer_parts = [part(far_outer + at, size) for at, size in pieces]
    outer_sums = [inward(array) for array in outer_parts]
    inner_parts = [part(far_inner + at, size) for at, size in halves]
    inner_sums = [inward(array) for array in inner_parts]
    to_outer, to_own, returned, direct = [None] * 3, [None] * 2, [None] * 3, [None] * 2

    def send_outer(at):
        to_outer[at] = across(step(outer_parts[at], outer_sums[at]))

    def send_inner(at):
        to_own[at] = across(step(inner_parts[at], inner_sums[at]))
        direct[at] = inward(after(near_parts[at], chain[-1]))

    def send_back(at):
        returned[at] = outward(step(near_pieces[at], to_outer[at]))

    send_outer(0)
    send_outer(1)
    projected.append(chain[-1])
    near_parts = [part(near + at, size) for at, size in halves]
    near_pieces = [near_parts[0][:, :fourth], near_parts[0][:, fourth:], near_parts[1]]
    send_outer(2)
    send_back(0)
    send_back(1)
    mine = part(own, quarter)
    send_inner(0)
    left = step(mine[:, :half], jnp.concatenate(returned[:2], axis=1))
    send_inner(1)
    send_back(2)
    left = step(left, to_own[0], direct[0])
    right = step(mine[:, half:], returned[2], to_own[1], direct[1])
    return jnp.concatenate([left, right], axis=1)


def body(mesh, queries, keys, values, out_weight, storm_mask):
    place = lax.axis_index("ctx")
    heads = queries.shape[1] // HDIM
    shared_head = lax.axis_index("tp") * heads // GQ
    packed = pack_head(keys, values, shared_head)
    attended = attend(queries, packed, place, mesh.shape["ctx"], storm_mask)
    if mesh.shape["tp"] == 4:
        return line_sum(attended, out_weight)
    partial = project(attended, out_weight, jnp.int32(0), out_weight.shape[1])
    return lax.psum_scatter(partial, "tp", scatter_dimension=1, tiled=True)


def solution(mesh):
    placed = (P("ctx", "tp"), P("ctx", None), P("ctx", None), P("tp", None), P())
    return jax.shard_map(
        functools.partial(body, mesh),
        mesh=mesh,
        in_specs=placed,
        out_specs=P("ctx", "tp"),
        check_vma=False,
    )
```

```python
import functools
import math

import jax
import jax.numpy as jnp
from jax import lax
from jax.experimental import pallas as pl
from jax.experimental.pallas import tpu as pltpu
from jax.sharding import PartitionSpec as P

HDIM = 128
BLOCK = 128
GQ = 8
TILE = 512
EXPONENT = HDIM ** (-0.5) * math.log2(math.e)
VMEM_LIMIT = 48 * 1024 * 1024


def pack_head(keys, values, head):
    return jnp.concatenate(
        [lax.dynamic_slice_in_dim(array, head * HDIM, HDIM, 1) for array in (keys, values)], axis=1
    )


def choose_blocks(place, swaps, owners, row, per_device, mask_ref, chosen):
    def choose(slot, found):
        owner = place ^ swaps[slot] if swaps else slot
        for part in range(per_device):
            here = mask_ref[row, owner * per_device + part] == 1
            chosen[found] = slot * per_device + part
            found = found + here.astype(jnp.int32)
        return found

    if not swaps:
        return lax.fori_loop(0, owners, choose, jnp.int32(0))
    found = jnp.int32(0)
    for slot in range(owners):
        found = choose(slot, found)
    return found


def attention_kernel(parts, swaps, first, place_ref, mask_ref, query_ref, *refs):
    if first:
        own_hbm, *refs = refs
        kv_refs = refs[:parts]
        query_out, peaks, totals, sums, kv, peak, scores, chosen, arrived = refs[parts:]
        loads = [pltpu.make_async_copy(query_ref, query_out, arrived.at[0])]
        if swaps:
            loads.append(pltpu.make_async_copy(own_hbm, kv.at[0], arrived.at[1]))
        for load in loads:
            load.start()
        at = len(loads) - 1
        peaks[...] = jnp.full(peaks.shape, -1e30, jnp.float32)
        totals[...] = jnp.zeros(totals.shape, jnp.float32)
        sums[...] = jnp.zeros(sums.shape, jnp.float32)
    else:
        peaks, totals_in, sums_in, *refs = refs
        kv_refs = refs[:parts]
        weight_hbm, out_ref, partial_ref, kv, peak, scores, totals, sums, *refs = refs[parts:]
        weight, chosen, arrived = refs
        columns = weight.shape[1]
        column = pl.multiple_of(place_ref[1] * columns, columns)
        loads = [pltpu.make_async_copy(weight_hbm.at[:, pl.ds(column, columns)], weight, arrived)]
        loads[0].start()
        at = 0
    for ref in kv_refs:
        count = ref.shape[0]
        kv[at : at + count] = ref[...]
        at += count
    if first:
        for load in loads:
            load.wait()
        query_ref = query_out
    rows, width = query_ref.shape
    heads = width // HDIM
    per_device = rows // BLOCK
    place = place_ref[0]
    owners = kv.shape[0]

    for block in range(per_device):
        top = slice(block * BLOCK, (block + 1) * BLOCK)
        found = choose_blocks(
            place, swaps, owners, place * per_device + block, per_device, mask_ref, chosen
        )

        def tiles(start, count):
            for number in range(count):
                index = chosen[start + number]
                here = pl.multiple_of((index % per_device) * BLOCK, BLOCK)
                yield index // per_device, pl.ds(here, BLOCK)

        def score(start, count):
            keys = [kv[slot, here, :HDIM] for slot, here in tiles(start, count)]
            keys = jnp.concatenate(keys, axis=0)
            for head in range(heads):
                query = query_ref[top, head * HDIM : (head + 1) * HDIM]
                found_here = lax.dot_general(
                    query, keys, (((1,), (1,)), ((), ())), preferred_element_type=jnp.float32
                )
                highest = peak[head]
                for number in range(count):
                    part = found_here[:, number * BLOCK : (number + 1) * BLOCK]
                    scores[start + number, head] = part
                    highest = jnp.maximum(highest, part)
                peak[head] = highest

        def weigh(start, count):
            values = [kv[slot, here, HDIM:] for slot, here in tiles(start, count)]
            values = jnp.concatenate(values, axis=0)
            for head in range(heads):
                weights = [
                    jnp.exp2((scores[start + number, head] - peak[head]) * EXPONENT)
                    for number in range(count)
                ]
                totals[block, head] += sum(weights[1:], weights[0])
                weights = jnp.concatenate([w.astype(jnp.bfloat16) for w in weights], axis=1)
                sums[block, head] += jnp.dot(weights, values, preferred_element_type=jnp.float32)

        def over_blocks(work):
            def four(number, carry):
                work(4 * number, 4)
                return carry

            lax.fori_loop(0, found // 4, four, 0)

            @pl.when((found & 2) == 2)
            def _():
                work(found // 4 * 4, 2)

            @pl.when((found & 1) == 1)
            def _():
                work(found - 1, 1)

        peak[...] = peaks[block]
        over_blocks(score)
        for head in range(heads):
            highest = jnp.max(peak[head], axis=1, keepdims=True)
            peak[head] = jnp.broadcast_to(highest, (BLOCK, BLOCK))
            if first:
                peaks[block, head] = peak[head]
            else:
                factor = jnp.exp2((peaks[block, head] - peak[head]) * EXPONENT)
                totals[block, head] = totals_in[block, head] * factor
                sums[block, head] = sums_in[block, head] * factor
        over_blocks(weigh)

        if not first:
            for head in range(heads):
                norm = jnp.sum(totals[block, head], axis=1, keepdims=True)
                out_ref[top, head * HDIM : (head + 1) * HDIM] = (sums[block, head] / norm).astype(
                    jnp.bfloat16
                )

    if not first:
        loads[0].wait()
        partial_ref[...] = jnp.dot(
            out_ref[...], weight[...], preferred_element_type=jnp.float32
        ).astype(jnp.bfloat16)


def attention_part(first, swaps, count, place, storm_mask, query, state, parts, *projection):
    rows, width = query.shape
    heads = width // HDIM
    blocks = count * (rows // BLOCK)
    vmem = pl.BlockSpec(memory_space=pltpu.VMEM)
    hbm = pl.BlockSpec(memory_space=pl.ANY)
    running = (rows // BLOCK, heads, BLOCK, BLOCK)
    taken = jax.ShapeDtypeStruct((rows, width), jnp.bfloat16)
    scratch = [
        pltpu.VMEM((count, rows, 2 * HDIM), jnp.bfloat16),
        pltpu.VMEM((heads, BLOCK, BLOCK), jnp.float32),
        pltpu.VMEM((blocks, heads, BLOCK, BLOCK), jnp.float32),
    ]
    if first:
        specs = [hbm, hbm] + [vmem] * len(parts)
        out_shape = [taken] + [jax.ShapeDtypeStruct(running, jnp.float32)] * 3
    else:
        weight, column, columns = projection
        place = jnp.stack([place, column // columns])
        parts = [*parts, weight]
        specs = [vmem] * (3 + len(parts)) + [hbm]
        out_shape = [taken, jax.ShapeDtypeStruct((rows, columns), jnp.bfloat16)]
        scratch += [pltpu.VMEM(running, jnp.float32)] * 2
        scratch += [pltpu.VMEM((weight.shape[0], columns), jnp.bfloat16)]
    scratch += [pltpu.SMEM((blocks + 1,), jnp.int32)]
    scratch += [pltpu.SemaphoreType.DMA((2,)) if first else pltpu.SemaphoreType.DMA]
    return pl.pallas_call(
        functools.partial(attention_kernel, len(parts) - len(projection[:1]), swaps, first),
        grid_spec=pltpu.PrefetchScalarGridSpec(
            num_scalar_prefetch=2,
            grid=(1,),
            in_specs=specs,
            out_specs=[vmem] * len(out_shape),
            scratch_shapes=scratch,
        ),
        out_shape=out_shape,
        compiler_params=pltpu.CompilerParams(vmem_limit_bytes=VMEM_LIMIT),
        name="attend_first" if first else "attend_rest",
    )(place.astype(jnp.int32).reshape(-1), storm_mask, query, *state, *parts)


def attend(queries, packed, place, devices, storm_mask, *projection):
    if devices != 8:
        everyone = lax.all_gather(packed, "ctx", axis=0, tiled=False)
        state = attention_part(
            True, (), devices, place, storm_mask, queries, [packed], [everyone]
        )
        query, *state = state
        nothing = jnp.zeros_like(storm_mask)
        return attention_part(
            False, (), 1, place, nothing, query, state, [everyone[:1]], *projection
        )

    def swap(array, bits):
        return lax.ppermute(array, "ctx", [(i, i ^ bits) for i in range(devices)])

    near = [swap(packed[None], bits) for bits in (6, 2, 4)]
    query, *state = attention_part(
        True, (0, 1), 2, place, storm_mask, queries, [packed], [swap(packed[None], 1)]
    )
    other = [swap(array, 1) for array in near]
    return attention_part(
        False, (6, 2, 4, 7, 3, 5), 6, place, storm_mask, query, state, near + other, *projection
    )


def project_kernel(first_ref, attended_ref, weight_ref, out_ref):
    out_ref[...] = jnp.dot(
        attended_ref[...], weight_ref[...], preferred_element_type=jnp.float32
    ).astype(jnp.bfloat16)


def project(attended, out_weight, first, columns):
    rows, depth = attended.shape
    tile = min(TILE, columns)
    return pl.pallas_call(
        project_kernel,
        grid_spec=pltpu.PrefetchScalarGridSpec(
            num_scalar_prefetch=1,
            grid=(columns // tile,),
            in_specs=[
                pl.BlockSpec((rows, depth), lambda i, first: (0, 0)),
                pl.BlockSpec((depth, tile), lambda i, first: (0, first[0] + i)),
            ],
            out_specs=pl.BlockSpec((rows, tile), lambda i, first: (0, i)),
        ),
        out_shape=jax.ShapeDtypeStruct((rows, columns), jnp.bfloat16),
        compiler_params=pltpu.CompilerParams(vmem_limit_bytes=VMEM_LIMIT),
        name="project",
    )((first // tile).astype(jnp.int32).reshape(1), attended, out_weight)


def after(array, *earlier):
    return lax.optimization_barrier((array, *earlier))[0]


def added(*arrays):
    wide = [array.astype(jnp.float32) for array in arrays]
    return functools.reduce(lambda a, b: a + b, wide).astype(jnp.bfloat16)


def line_sum(attend_now, out_weight):
    place = lax.axis_index("tp")
    quarter = out_weight.shape[1] // 4
    upper = place >= 2
    far_outer = jnp.where(upper, 0, 3) * quarter
    far_inner = jnp.where(upper, 1, 2) * quarter
    near = jnp.where(upper, 5 - place, 1 - place) * quarter
    own = place * quarter
    half = quarter // 2
    fourth = quarter // 4
    pieces = ((0, fourth), (fourth, fourth), (half, half))
    halves = ((0, half), (half, half))
    attended, partial = attend_now(far_outer, fourth)
    projected, chain = [partial], []

    def part(first, columns):
        source = after(attended, projected[-1]) if projected else attended
        projected.append(project(source, out_weight, first, columns))
        return projected[-1]

    def step(*arrays):
        first = after(arrays[0], chain[-1]) if chain else arrays[0]
        chain.append(added(first, *arrays[1:]))
        return chain[-1]

    def inward(array):
        return lax.ppermute(array, "tp", [(0, 1), (3, 2)])

    def across(array):
        return lax.ppermute(array, "tp", [(1, 2), (2, 1)])

    def outward(array):
        return lax.ppermute(array, "tp", [(1, 0), (2, 3)])

    outer_parts = [partial] + [part(far_outer + at, size) for at, size in pieces[1:]]
    outer_sums = [inward(array) for array in outer_parts]
    inner_parts = [part(far_inner + at, size) for at, size in halves]
    inner_sums = [inward(array) for array in inner_parts]
    to_outer, to_own, returned, direct = [None] * 3, [None] * 2, [None] * 3, [None] * 2

    def send_outer(at):
        to_outer[at] = across(step(outer_parts[at], outer_sums[at]))

    def send_inner(at):
        to_own[at] = across(step(inner_parts[at], inner_sums[at]))
        direct[at] = inward(after(near_parts[at], chain[-1]))

    def send_back(at):
        returned[at] = outward(step(near_pieces[at], to_outer[at]))

    send_outer(0)
    send_outer(1)
    projected.append(chain[-1])
    near_parts = [part(near + at, size) for at, size in halves]
    near_pieces = [near_parts[0][:, :fourth], near_parts[0][:, fourth:], near_parts[1]]
    send_outer(2)
    send_back(0)
    send_back(1)
    mine = part(own, quarter)
    send_inner(0)
    left = step(mine[:, :half], jnp.concatenate(returned[:2], axis=1))
    send_inner(1)
    send_back(2)
    left = step(left, to_own[0], direct[0])
    right = step(mine[:, half:], returned[2], to_own[1], direct[1])
    return jnp.concatenate([left, right], axis=1)


def body(mesh, queries, keys, values, out_weight, storm_mask):
    place = lax.axis_index("ctx")
    heads = queries.shape[1] // HDIM
    shared_head = lax.axis_index("tp") * heads // GQ
    packed = pack_head(keys, values, shared_head)

    def attend_now(first, columns):
        return attend(
            queries, packed, place, mesh.shape["ctx"], storm_mask, out_weight, first, columns
        )

    if mesh.shape["tp"] == 4:
        return line_sum(attend_now, out_weight)
    _, partial = attend_now(jnp.int32(0), out_weight.shape[1])
    return lax.psum_scatter(partial, "tp", scatter_dimension=1, tiled=True)


def solution(mesh):
    placed = (P("ctx", "tp"), P("ctx", None), P("ctx", None), P("tp", None), P())
    return jax.shard_map(
        functools.partial(body, mesh),
        mesh=mesh,
        in_specs=placed,
        out_specs=P("ctx", "tp"),
        check_vma=False,
    )
```

```python
import functools
import math

import jax
import jax.numpy as jnp
from jax import lax
from jax.experimental import pallas as pl
from jax.experimental.pallas import tpu as pltpu
from jax.sharding import PartitionSpec as P

HDIM = 128
BLOCK = 128
GQ = 8
TILE = 512
EXPONENT = HDIM ** (-0.5) * math.log2(math.e)
VMEM_LIMIT = 48 * 1024 * 1024


def pack_head(keys, values, head):
    return jnp.concatenate(
        [lax.dynamic_slice_in_dim(array, head * HDIM, HDIM, 1) for array in (keys, values)], axis=1
    )


def choose_blocks(place, swaps, owners, row, per_device, mask_ref, chosen):
    def choose(slot, found):
        owner = place ^ swaps[slot] if swaps else slot
        for part in range(per_device):
            here = mask_ref[row, owner * per_device + part] == 1
            chosen[found] = slot * per_device + part
            found = found + here.astype(jnp.int32)
        return found

    if not swaps:
        return lax.fori_loop(0, owners, choose, jnp.int32(0))
    found = jnp.int32(0)
    for slot in range(owners):
        found = choose(slot, found)
    return found


def attention_kernel(parts, swaps, first, place_ref, mask_ref, query_ref, *refs):
    if first:
        own_hbm, *refs = refs
        kv_refs = refs[:parts]
        query_out, peaks, totals, sums, kv, peak, scores, chosen, arrived = refs[parts:]
        loads = [pltpu.make_async_copy(query_ref, query_out, arrived.at[0])]
        if swaps:
            loads.append(pltpu.make_async_copy(own_hbm, kv.at[0], arrived.at[1]))
        for load in loads:
            load.start()
        at = len(loads) - 1
        peaks[...] = jnp.full(peaks.shape, -1e30, jnp.float32)
        totals[...] = jnp.zeros(totals.shape, jnp.float32)
        sums[...] = jnp.zeros(sums.shape, jnp.float32)
    else:
        peaks, totals_in, sums_in, *refs = refs
        kv_refs = refs[:parts]
        weight_hbm, out_ref, partial_ref, kv, peak, scores, totals, sums, *refs = refs[parts:]
        weight, chosen, arrived = refs
        columns = weight.shape[1]
        column = pl.multiple_of(place_ref[1] * columns, columns)
        loads = [pltpu.make_async_copy(weight_hbm.at[:, pl.ds(column, columns)], weight, arrived)]
        loads[0].start()
        at = 0
    for ref in kv_refs:
        count = ref.shape[0]
        kv[at : at + count] = ref[...]
        at += count
    if first:
        for load in loads:
            load.wait()
        query_ref = query_out
    rows, width = query_ref.shape
    heads = width // HDIM
    per_device = rows // BLOCK
    place = place_ref[0]
    owners = kv.shape[0]

    for block in range(per_device):
        top = slice(block * BLOCK, (block + 1) * BLOCK)
        found = choose_blocks(
            place, swaps, owners, place * per_device + block, per_device, mask_ref, chosen
        )

        def tiles(start, count):
            for number in range(count):
                index = chosen[start + number]
                here = pl.multiple_of((index % per_device) * BLOCK, BLOCK)
                yield index // per_device, pl.ds(here, BLOCK)

        def score(start, count):
            keys = [kv[slot, here, :HDIM] for slot, here in tiles(start, count)]
            keys = jnp.concatenate(keys, axis=0)
            for head in range(heads):
                query = query_ref[top, head * HDIM : (head + 1) * HDIM]
                found_here = lax.dot_general(
                    query, keys, (((1,), (1,)), ((), ())), preferred_element_type=jnp.float32
                )
                highest = peak[head]
                for number in range(count):
                    part = found_here[:, number * BLOCK : (number + 1) * BLOCK]
                    scores[start + number, head] = part
                    highest = jnp.maximum(highest, part)
                peak[head] = highest

        def weigh(start, count):
            values = [kv[slot, here, HDIM:] for slot, here in tiles(start, count)]
            values = jnp.concatenate(values, axis=0)
            for head in range(heads):
                weights = [
                    jnp.exp2((scores[start + number, head] - peak[head]) * EXPONENT)
                    for number in range(count)
                ]
                totals[block, head] += sum(weights[1:], weights[0])
                weights = jnp.concatenate([w.astype(jnp.bfloat16) for w in weights], axis=1)
                sums[block, head] += jnp.dot(weights, values, preferred_element_type=jnp.float32)

        def over_blocks(work):
            def four(number, carry):
                work(4 * number, 4)
                return carry

            lax.fori_loop(0, found // 4, four, 0)

            @pl.when((found & 2) == 2)
            def _():
                work(found // 4 * 4, 2)

            @pl.when((found & 1) == 1)
            def _():
                work(found - 1, 1)

        peak[...] = peaks[block]
        over_blocks(score)
        for head in range(heads):
            highest = jnp.max(peak[head], axis=1, keepdims=True)
            peak[head] = jnp.broadcast_to(highest, (BLOCK, BLOCK))
            if first:
                peaks[block, head] = peak[head]
            else:
                factor = jnp.exp2((peaks[block, head] - peak[head]) * EXPONENT)
                totals[block, head] = totals_in[block, head] * factor
                sums[block, head] = sums_in[block, head] * factor
        over_blocks(weigh)

        if not first:
            for head in range(heads):
                norm = jnp.sum(totals[block, head], axis=1, keepdims=True)
                out_ref[top, head * HDIM : (head + 1) * HDIM] = (sums[block, head] / norm).astype(
                    jnp.bfloat16
                )

    if not first:
        loads[0].wait()
        partial_ref[...] = jnp.dot(
            out_ref[...], weight[...], preferred_element_type=jnp.float32
        ).astype(jnp.bfloat16)


def attention_part(first, swaps, count, place, storm_mask, query, state, parts, *projection):
    rows, width = query.shape
    heads = width // HDIM
    blocks = count * (rows // BLOCK)
    vmem = pl.BlockSpec(memory_space=pltpu.VMEM)
    hbm = pl.BlockSpec(memory_space=pl.ANY)
    running = (rows // BLOCK, heads, BLOCK, BLOCK)
    taken = jax.ShapeDtypeStruct((rows, width), jnp.bfloat16)
    scratch = [
        pltpu.VMEM((count, rows, 2 * HDIM), jnp.bfloat16),
        pltpu.VMEM((heads, BLOCK, BLOCK), jnp.float32),
        pltpu.VMEM((blocks, heads, BLOCK, BLOCK), jnp.float32),
    ]
    if first:
        specs = [hbm, hbm] + [vmem] * len(parts)
        out_shape = [taken] + [jax.ShapeDtypeStruct(running, jnp.float32)] * 3
    else:
        weight, column, columns = projection
        place = jnp.stack([place, column // columns])
        parts = [*parts, weight]
        specs = [vmem] * (3 + len(parts)) + [hbm]
        out_shape = [taken, jax.ShapeDtypeStruct((rows, columns), jnp.bfloat16)]
        scratch += [pltpu.VMEM(running, jnp.float32)] * 2
        scratch += [pltpu.VMEM((weight.shape[0], columns), jnp.bfloat16)]
    scratch += [pltpu.SMEM((blocks + 1,), jnp.int32)]
    scratch += [pltpu.SemaphoreType.DMA((2,)) if first else pltpu.SemaphoreType.DMA]
    return pl.pallas_call(
        functools.partial(attention_kernel, len(parts) - len(projection[:1]), swaps, first),
        grid_spec=pltpu.PrefetchScalarGridSpec(
            num_scalar_prefetch=2,
            grid=(1,),
            in_specs=specs,
            out_specs=[vmem] * len(out_shape),
            scratch_shapes=scratch,
        ),
        out_shape=out_shape,
        compiler_params=pltpu.CompilerParams(vmem_limit_bytes=VMEM_LIMIT),
        name="attend_first" if first else "attend_rest",
    )(place.astype(jnp.int32).reshape(-1), storm_mask, query, *state, *parts)


def attend(queries, packed, place, devices, storm_mask, *projection):
    if devices != 8:
        everyone = lax.all_gather(packed, "ctx", axis=0, tiled=False)
        state = attention_part(
            True, (), devices, place, storm_mask, queries, [packed], [everyone]
        )
        query, *state = state
        nothing = jnp.zeros_like(storm_mask)
        return attention_part(
            False, (), 1, place, nothing, query, state, [everyone[:1]], *projection
        )

    def swap(array, bits):
        return lax.ppermute(array, "ctx", [(i, i ^ bits) for i in range(devices)])

    near = [swap(packed[None], bits) for bits in (6, 2, 4)]
    query, *state = attention_part(
        True, (0, 1), 2, place, storm_mask, queries, [packed], [swap(packed[None], 1)]
    )
    other = [swap(array, 1) for array in near]
    return attention_part(
        False, (6, 2, 4, 7, 3, 5), 6, place, storm_mask, query, state, near + other, *projection
    )


def project_kernel(first_ref, attended_ref, weight_ref, out_ref):
    out_ref[...] = jnp.dot(
        attended_ref[...], weight_ref[...], preferred_element_type=jnp.float32
    ).astype(jnp.bfloat16)


def project(attended, out_weight, first, columns):
    rows, depth = attended.shape
    tile = min(TILE, columns)
    return pl.pallas_call(
        project_kernel,
        grid_spec=pltpu.PrefetchScalarGridSpec(
            num_scalar_prefetch=1,
            grid=(columns // tile,),
            in_specs=[
                pl.BlockSpec((rows, depth), lambda i, first: (0, 0)),
                pl.BlockSpec((depth, tile), lambda i, first: (0, first[0] + i)),
            ],
            out_specs=pl.BlockSpec((rows, tile), lambda i, first: (0, i)),
        ),
        out_shape=jax.ShapeDtypeStruct((rows, columns), jnp.bfloat16),
        compiler_params=pltpu.CompilerParams(vmem_limit_bytes=VMEM_LIMIT),
        name="project",
    )((first // tile).astype(jnp.int32).reshape(1), attended, out_weight)


def after(array, *earlier):
    return lax.optimization_barrier((array, *earlier))[0]


def added(*arrays):
    wide = [array.astype(jnp.float32) for array in arrays]
    return functools.reduce(lambda a, b: a + b, wide).astype(jnp.bfloat16)


def line_sum(attend_now, out_weight):
    place = lax.axis_index("tp")
    quarter = out_weight.shape[1] // 4
    upper = place >= 2
    far_outer = jnp.where(upper, 0, 3) * quarter
    far_inner = jnp.where(upper, 1, 2) * quarter
    near = jnp.where(upper, 5 - place, 1 - place) * quarter
    own = place * quarter
    half = quarter // 2
    fourth = quarter // 4
    pieces = ((0, fourth), (fourth, fourth), (half, half))
    halves = ((0, half), (half, half))
    attended, partial = attend_now(far_outer, fourth)
    projected, chain = [partial], []

    def part(first, columns):
        source = after(attended, projected[-1]) if projected else attended
        projected.append(project(source, out_weight, first, columns))
        return projected[-1]

    def step(*arrays):
        first = after(arrays[0], chain[-1]) if chain else arrays[0]
        chain.append(added(first, *arrays[1:]))
        return chain[-1]

    def inward(array):
        return lax.ppermute(array, "tp", [(0, 1), (3, 2)])

    def across(array):
        return lax.ppermute(array, "tp", [(1, 2), (2, 1)])

    def outward(array):
        return lax.ppermute(array, "tp", [(1, 0), (2, 3)])

    outer_parts = [partial] + [part(far_outer + at, size) for at, size in pieces[1:]]
    outer_sums = [inward(array) for array in outer_parts]
    inner_parts = [part(far_inner + at, size) for at, size in halves]
    inner_sums = [inward(array) for array in inner_parts]
    to_outer, to_own, returned, direct = [None] * 3, [None] * 2, [None] * 3, [None] * 2

    def send_outer(at):
        to_outer[at] = across(step(outer_parts[at], outer_sums[at]))

    def send_inner(at):
        to_own[at] = across(step(inner_parts[at], inner_sums[at]))

    def send_direct(at):
        direct[at] = inward(after(near_parts[at], chain[-1]))

    def send_back(at):
        returned[at] = outward(step(near_pieces[at], to_outer[at]))

    send_outer(0)
    send_outer(1)
    projected.append(chain[-1])
    near_parts = [part(near + at, size) for at, size in halves]
    near_pieces = [near_parts[0][:, :fourth], near_parts[0][:, fourth:], near_parts[1]]
    send_outer(2)
    send_back(0)
    send_back(1)
    mine = part(own, quarter)
    send_inner(0)
    send_direct(0)
    left = step(mine[:, :half], jnp.concatenate(returned[:2], axis=1))
    send_inner(1)
    send_back(2)
    ends = (slice(0, fourth), slice(fourth, half))
    last = [inward(after(near_parts[1], chain[-1])[:, end]) for end in ends]
    left = step(left, to_own[0], direct[0])
    result = jnp.concatenate([left, mine[:, half:]], axis=1)
    for end, arrived in zip(ends, last):
        rest = after(result, left)[:, half + end.start : half + end.stop]
        final = added(rest, returned[2][:, end], to_own[1][:, end], arrived)
        result = lax.dynamic_update_slice(result, final, (0, half + end.start))
    return result


def body(mesh, queries, keys, values, out_weight, storm_mask):
    place = lax.axis_index("ctx")
    heads = queries.shape[1] // HDIM
    shared_head = lax.axis_index("tp") * heads // GQ
    packed = pack_head(keys, values, shared_head)

    def attend_now(first, columns):
        return attend(
            queries, packed, place, mesh.shape["ctx"], storm_mask, out_weight, first, columns
        )

    if mesh.shape["tp"] == 4:
        return line_sum(attend_now, out_weight)
    _, partial = attend_now(jnp.int32(0), out_weight.shape[1])
    return lax.psum_scatter(partial, "tp", scatter_dimension=1, tiled=True)


def solution(mesh):
    placed = (P("ctx", "tp"), P("ctx", None), P("ctx", None), P("tp", None), P())
    return jax.shard_map(
        functools.partial(body, mesh),
        mesh=mesh,
        in_specs=placed,
        out_specs=P("ctx", "tp"),
        check_vma=False,
    )
```

```python
import functools
import math

import jax
import jax.numpy as jnp
from jax import lax
from jax.experimental import pallas as pl
from jax.experimental.pallas import tpu as pltpu
from jax.sharding import PartitionSpec as P

HDIM = 128
BLOCK = 128
GQ = 8
TILE = 512
EXPONENT = HDIM ** (-0.5) * math.log2(math.e)
VMEM_LIMIT = 48 * 1024 * 1024


def pack_head(keys, values, head):
    return jnp.concatenate(
        [lax.dynamic_slice_in_dim(array, head * HDIM, HDIM, 1) for array in (keys, values)], axis=1
    )


def choose_blocks(place, swaps, owners, row, per_device, mask_ref, chosen):
    def choose(slot, found):
        owner = place ^ swaps[slot] if swaps else slot
        for part in range(per_device):
            here = mask_ref[row, owner * per_device + part] == 1
            chosen[found] = slot * per_device + part
            found = found + here.astype(jnp.int32)
        return found

    if not swaps:
        return lax.fori_loop(0, owners, choose, jnp.int32(0))
    found = jnp.int32(0)
    for slot in range(owners):
        found = choose(slot, found)
    return found


def attention_kernel(parts, swaps, first, chosen_rows, place_ref, mask_ref, query_ref, *refs):
    if first:
        own_hbm, *refs = refs
        kv_refs = refs[:parts]
        query_out, peaks, totals, sums, kv, peak, scores, chosen, arrived = refs[parts:]
        loads = [pltpu.make_async_copy(query_ref, query_out, arrived.at[0])]
        if swaps:
            loads.append(pltpu.make_async_copy(own_hbm, kv.at[0], arrived.at[1]))
        for load in loads:
            load.start()
        at = len(loads) - 1
        peaks[...] = jnp.full(peaks.shape, -1e30, jnp.float32)
        totals[...] = jnp.zeros(totals.shape, jnp.float32)
        sums[...] = jnp.zeros(sums.shape, jnp.float32)
    else:
        peaks, totals_in, sums_in, *refs = refs
        kv_refs = refs[:parts]
        weight_hbm, out_ref, partial_ref, kv, peak, scores, totals, sums, *refs = refs[parts:]
        weight, chosen, arrived = refs
        columns = weight.shape[1]
        column = pl.multiple_of(place_ref[1] * columns, columns)
        loads = [pltpu.make_async_copy(weight_hbm.at[:, pl.ds(column, columns)], weight, arrived)]
        loads[0].start()
        at = 0
    for ref in kv_refs:
        count = ref.shape[0]
        kv[at : at + count] = ref[...]
        at += count
    if first:
        for load in loads:
            load.wait()
        query_ref = query_out
    rows, width = query_ref.shape
    heads = width // HDIM
    per_device = rows // BLOCK
    place = place_ref[0]
    owners = kv.shape[0]

    for block in chosen_rows:
        top = slice(block * BLOCK, (block + 1) * BLOCK)
        found = choose_blocks(
            place, swaps, owners, place * per_device + block, per_device, mask_ref, chosen
        )

        def tiles(start, count):
            for number in range(count):
                index = chosen[start + number]
                here = pl.multiple_of((index % per_device) * BLOCK, BLOCK)
                yield index // per_device, pl.ds(here, BLOCK)

        def score(start, count):
            keys = [kv[slot, here, :HDIM] for slot, here in tiles(start, count)]
            keys = jnp.concatenate(keys, axis=0)
            for head in range(heads):
                query = query_ref[top, head * HDIM : (head + 1) * HDIM]
                found_here = lax.dot_general(
                    query, keys, (((1,), (1,)), ((), ())), preferred_element_type=jnp.float32
                )
                highest = peak[head]
                for number in range(count):
                    part = found_here[:, number * BLOCK : (number + 1) * BLOCK]
                    scores[start + number, head] = part
                    highest = jnp.maximum(highest, part)
                peak[head] = highest

        def weigh(start, count):
            values = [kv[slot, here, HDIM:] for slot, here in tiles(start, count)]
            values = jnp.concatenate(values, axis=0)
            for head in range(heads):
                weights = [
                    jnp.exp2((scores[start + number, head] - peak[head]) * EXPONENT)
                    for number in range(count)
                ]
                totals[block, head] += sum(weights[1:], weights[0])
                weights = jnp.concatenate([w.astype(jnp.bfloat16) for w in weights], axis=1)
                sums[block, head] += jnp.dot(weights, values, preferred_element_type=jnp.float32)

        def over_blocks(work):
            def four(number, carry):
                work(4 * number, 4)
                return carry

            lax.fori_loop(0, found // 4, four, 0)

            @pl.when((found & 2) == 2)
            def _():
                work(found // 4 * 4, 2)

            @pl.when((found & 1) == 1)
            def _():
                work(found - 1, 1)

        peak[...] = peaks[block]
        over_blocks(score)
        for head in range(heads):
            highest = jnp.max(peak[head], axis=1, keepdims=True)
            peak[head] = jnp.broadcast_to(highest, (BLOCK, BLOCK))
            if first:
                peaks[block, head] = peak[head]
            else:
                factor = jnp.exp2((peaks[block, head] - peak[head]) * EXPONENT)
                totals[block, head] = totals_in[block, head] * factor
                sums[block, head] = sums_in[block, head] * factor
        over_blocks(weigh)

        if not first:
            for head in range(heads):
                norm = jnp.sum(totals[block, head], axis=1, keepdims=True)
                out_ref[:, head * HDIM : (head + 1) * HDIM] = (sums[block, head] / norm).astype(
                    jnp.bfloat16
                )

    if not first:
        loads[0].wait()
        partial_ref[...] = jnp.dot(
            out_ref[...], weight[...], preferred_element_type=jnp.float32
        ).astype(jnp.bfloat16)


def attention_part(first, chosen_rows, swaps, count, place, storm_mask, query, state, parts, *projection):
    rows, width = query.shape
    heads = width // HDIM
    blocks = count * (rows // BLOCK)
    vmem = pl.BlockSpec(memory_space=pltpu.VMEM)
    hbm = pl.BlockSpec(memory_space=pl.ANY)
    running = (rows // BLOCK, heads, BLOCK, BLOCK)
    taken = jax.ShapeDtypeStruct((rows, width), jnp.bfloat16)
    scratch = [
        pltpu.VMEM((count, rows, 2 * HDIM), jnp.bfloat16),
        pltpu.VMEM((heads, BLOCK, BLOCK), jnp.float32),
        pltpu.VMEM((blocks, heads, BLOCK, BLOCK), jnp.float32),
    ]
    if first:
        specs = [hbm, hbm] + [vmem] * len(parts)
        out_shape = [taken] + [jax.ShapeDtypeStruct(running, jnp.float32)] * 3
    else:
        weight, column, columns = projection
        place = jnp.stack([place, column // columns])
        parts = [*parts, weight]
        specs = [vmem] * (3 + len(parts)) + [hbm]
        out_shape = [
            jax.ShapeDtypeStruct((BLOCK, wide), jnp.bfloat16) for wide in (width, columns)
        ]
        scratch += [pltpu.VMEM(running, jnp.float32)] * 2
        scratch += [pltpu.VMEM((weight.shape[0], columns), jnp.bfloat16)]
    scratch += [pltpu.SMEM((blocks + 1,), jnp.int32)]
    scratch += [pltpu.SemaphoreType.DMA((2,)) if first else pltpu.SemaphoreType.DMA]
    return pl.pallas_call(
        functools.partial(attention_kernel, len(parts) - len(projection[:1]), swaps, first, chosen_rows),
        grid_spec=pltpu.PrefetchScalarGridSpec(
            num_scalar_prefetch=2,
            grid=(1,),
            in_specs=specs,
            out_specs=[vmem] * len(out_shape),
            scratch_shapes=scratch,
        ),
        out_shape=out_shape,
        compiler_params=pltpu.CompilerParams(vmem_limit_bytes=VMEM_LIMIT),
        name="attend_first" if first else "attend_rest",
    )(place.astype(jnp.int32).reshape(-1), storm_mask, query, *state, *parts)


def attend(queries, packed, place, devices, storm_mask, *projection):
    every = tuple(range(queries.shape[0] // BLOCK))
    if devices != 8:
        everyone = lax.all_gather(packed, "ctx", axis=0, tiled=False)
        state = attention_part(
            True, every, (), devices, place, storm_mask, queries, [packed], [everyone]
        )
        query, *state = state
        nothing = jnp.zeros_like(storm_mask)
        swaps, parts, storm_mask = (), [everyone[:1]], nothing
    else:

        def swap(array, bits):
            return lax.ppermute(array, "ctx", [(i, i ^ bits) for i in range(devices)])

        near = [swap(packed[None], bits) for bits in (6, 2, 4)]
        query, *state = attention_part(
            True, every, (0, 1), 2, place, storm_mask, queries, [packed], [swap(packed[None], 1)]
        )
        swaps, parts = (6, 2, 4, 7, 3, 5), near + [swap(array, 1) for array in near]
    attended, partials = [], []
    for block in every:
        if partials:
            query = after(query, partials[-1])
        rows, partial = attention_part(
            False, (block,), swaps, len(swaps) or 1, place, storm_mask, query, state, parts, *projection
        )
        attended.append(rows)
        partials.append(partial)
    return attended, partials


def project_kernel(first_ref, *refs):
    *attended_refs, weight_ref, out_ref = refs
    at = 0
    for ref in attended_refs:
        rows = ref.shape[0]
        out_ref[at : at + rows] = jnp.dot(
            ref[...], weight_ref[...], preferred_element_type=jnp.float32
        ).astype(jnp.bfloat16)
        at += rows


def project(attended, out_weight, first, columns):
    depth = out_weight.shape[0]
    rows = sum(array.shape[0] for array in attended)
    tile = min(TILE, columns)
    return pl.pallas_call(
        project_kernel,
        grid_spec=pltpu.PrefetchScalarGridSpec(
            num_scalar_prefetch=1,
            grid=(columns // tile,),
            in_specs=[pl.BlockSpec(array.shape, lambda i, first: (0, 0)) for array in attended]
            + [pl.BlockSpec((depth, tile), lambda i, first: (0, first[0] + i))],
            out_specs=pl.BlockSpec((rows, tile), lambda i, first: (0, i)),
        ),
        out_shape=jax.ShapeDtypeStruct((rows, columns), jnp.bfloat16),
        compiler_params=pltpu.CompilerParams(vmem_limit_bytes=VMEM_LIMIT),
        name="project",
    )((first // tile).astype(jnp.int32).reshape(1), *attended, out_weight)


def after(array, *earlier):
    return lax.optimization_barrier((array, *earlier))[0]


def added(*arrays):
    wide = [array.astype(jnp.float32) for array in arrays]
    return functools.reduce(lambda a, b: a + b, wide).astype(jnp.bfloat16)


def line_sum(attend_now, out_weight):
    place = lax.axis_index("tp")
    quarter = out_weight.shape[1] // 4
    upper = place >= 2
    far_outer = jnp.where(upper, 0, 3) * quarter
    far_inner = jnp.where(upper, 1, 2) * quarter
    near = jnp.where(upper, 5 - place, 1 - place) * quarter
    own = place * quarter
    half = quarter // 2
    fourth = quarter // 4
    halves = ((0, half), (half, half))
    attended, partials = attend_now(far_outer, half)
    projected, chain = [partials[-1]], []
    ahead = partials[0].shape[0]

    def part(first, columns):
        source = [after(attended[0], projected[-1]), *attended[1:]]
        projected.append(project(source, out_weight, first, columns))
        return projected[-1]

    def step(*arrays):
        first = after(arrays[0], chain[-1]) if chain else arrays[0]
        chain.append(added(first, *arrays[1:]))
        return chain[-1]

    def inward(array):
        return lax.ppermute(array, "tp", [(0, 1), (3, 2)])

    def across(array):
        return lax.ppermute(array, "tp", [(1, 2), (2, 1)])

    def outward(array):
        return lax.ppermute(array, "tp", [(1, 0), (2, 3)])

    outer_parts = [*partials, part(far_outer + half, half)]
    outer_sums = [inward(array) for array in outer_parts]
    inner_parts = [part(far_inner + at, size) for at, size in halves]
    inner_sums = [inward(array) for array in inner_parts]
    to_outer, to_own, returned, direct = [None] * 3, [None] * 2, [None] * 3, [None] * 2

    def send_outer(at):
        to_outer[at] = across(step(outer_parts[at], outer_sums[at]))

    def send_inner(at):
        to_own[at] = across(step(inner_parts[at], inner_sums[at]))
        direct[at] = inward(after(near_parts[at], chain[-1]))

    def send_back(at):
        returned[at] = outward(step(near_pieces[at], to_outer[at]))

    send_outer(0)
    send_outer(1)
    projected.append(chain[-1])
    near_parts = [part(near + at, size) for at, size in halves]
    near_pieces = [near_parts[0][:ahead], near_parts[0][ahead:], near_parts[1]]
    send_outer(2)
    send_back(0)
    send_back(1)
    mine = part(own, quarter)
    send_inner(0)
    left = step(mine[:, :half], jnp.concatenate(returned[:2], axis=0))
    send_inner(1)
    send_back(2)
    left = step(left, to_own[0], direct[0])
    right = step(mine[:, half:], returned[2], to_own[1], direct[1])
    return jnp.concatenate([left, right], axis=1)


def body(mesh, queries, keys, values, out_weight, storm_mask):
    place = lax.axis_index("ctx")
    heads = queries.shape[1] // HDIM
    shared_head = lax.axis_index("tp") * heads // GQ
    packed = pack_head(keys, values, shared_head)

    def attend_now(first, columns):
        return attend(
            queries, packed, place, mesh.shape["ctx"], storm_mask, out_weight, first, columns
        )

    if mesh.shape["tp"] == 4:
        return line_sum(attend_now, out_weight)
    _, partials = attend_now(jnp.int32(0), out_weight.shape[1])
    partial = jnp.concatenate(partials, axis=0)
    return lax.psum_scatter(partial, "tp", scatter_dimension=1, tiled=True)


def solution(mesh):
    placed = (P("ctx", "tp"), P("ctx", None), P("ctx", None), P("tp", None), P())
    return jax.shard_map(
        functools.partial(body, mesh),
        mesh=mesh,
        in_specs=placed,
        out_specs=P("ctx", "tp"),
        check_vma=False,
    )
```

```python
import functools
import math

import jax
import jax.numpy as jnp
from jax import lax
from jax.experimental import pallas as pl
from jax.experimental.pallas import tpu as pltpu
from jax.sharding import PartitionSpec as P

HDIM = 128
BLOCK = 128
GQ = 8
TILE = 512
EXPONENT = HDIM ** (-0.5) * math.log2(math.e)
VMEM_LIMIT = 48 * 1024 * 1024


def pack_head(keys, values, head):
    return jnp.concatenate(
        [lax.dynamic_slice_in_dim(array, head * HDIM, HDIM, 1) for array in (keys, values)], axis=1
    )


def choose_blocks(place, swaps, owners, row, per_device, mask_ref, chosen):
    def choose(slot, found):
        owner = place ^ swaps[slot] if swaps else slot
        for part in range(per_device):
            here = mask_ref[row, owner * per_device + part] == 1
            chosen[found] = slot * per_device + part
            found = found + here.astype(jnp.int32)
        return found

    if not swaps:
        return lax.fori_loop(0, owners, choose, jnp.int32(0))
    found = jnp.int32(0)
    for slot in range(owners):
        found = choose(slot, found)
    return found


def attention_kernel(parts, swaps, first, chosen_rows, place_ref, mask_ref, query_ref, *refs):
    if first:
        own_hbm, *refs = refs
        kv_refs = refs[:parts]
        query_out, peaks, totals, sums, kv, peak, scores, chosen, arrived = refs[parts:]
        loads = [pltpu.make_async_copy(query_ref, query_out, arrived.at[0])]
        if swaps:
            loads.append(pltpu.make_async_copy(own_hbm, kv.at[0], arrived.at[1]))
        for load in loads:
            load.start()
        at = len(loads) - 1
        peaks[...] = jnp.full(peaks.shape, -1e30, jnp.float32)
        totals[...] = jnp.zeros(totals.shape, jnp.float32)
        sums[...] = jnp.zeros(sums.shape, jnp.float32)
    else:
        peaks, totals_in, sums_in, *refs = refs
        kv_refs = refs[:parts]
        weight_hbm, out_ref, partial_ref, kv, peak, scores, totals, sums, *refs = refs[parts:]
        weight, chosen, arrived = refs
        columns = weight.shape[1]
        column = pl.multiple_of(place_ref[1] * columns, columns)
        loads = [pltpu.make_async_copy(weight_hbm.at[:, pl.ds(column, columns)], weight, arrived)]
        loads[0].start()
        at = 0
    for ref in kv_refs:
        count = ref.shape[0]
        kv[at : at + count] = ref[...]
        at += count
    if first:
        for load in loads:
            load.wait()
        query_ref = query_out
    rows, width = query_ref.shape
    heads = width // HDIM
    per_device = rows // BLOCK
    place = place_ref[0]
    owners = kv.shape[0]

    for block in chosen_rows:
        top = slice(block * BLOCK, (block + 1) * BLOCK)
        found = choose_blocks(
            place, swaps, owners, place * per_device + block, per_device, mask_ref, chosen
        )

        def tiles(start, count):
            for number in range(count):
                index = chosen[start + number]
                here = pl.multiple_of((index % per_device) * BLOCK, BLOCK)
                yield index // per_device, pl.ds(here, BLOCK)

        def score(start, count):
            keys = [kv[slot, here, :HDIM] for slot, here in tiles(start, count)]
            keys = jnp.concatenate(keys, axis=0)
            for head in range(heads):
                query = query_ref[top, head * HDIM : (head + 1) * HDIM]
                found_here = lax.dot_general(
                    query, keys, (((1,), (1,)), ((), ())), preferred_element_type=jnp.float32
                )
                highest = peak[head]
                for number in range(count):
                    part = found_here[:, number * BLOCK : (number + 1) * BLOCK]
                    scores[start + number, head] = part
                    highest = jnp.maximum(highest, part)
                peak[head] = highest

        def weigh(start, count):
            values = [kv[slot, here, HDIM:] for slot, here in tiles(start, count)]
            values = jnp.concatenate(values, axis=0)
            for head in range(heads):
                weights = [
                    jnp.exp2((scores[start + number, head] - peak[head]) * EXPONENT)
                    for number in range(count)
                ]
                totals[block, head] += sum(weights[1:], weights[0])
                weights = jnp.concatenate([w.astype(jnp.bfloat16) for w in weights], axis=1)
                sums[block, head] += jnp.dot(weights, values, preferred_element_type=jnp.float32)

        def over_blocks(work):
            def four(number, carry):
                work(4 * number, 4)
                return carry

            lax.fori_loop(0, found // 4, four, 0)

            @pl.when((found & 2) == 2)
            def _():
                work(found // 4 * 4, 2)

            @pl.when((found & 1) == 1)
            def _():
                work(found - 1, 1)

        peak[...] = peaks[block]
        over_blocks(score)
        for head in range(heads):
            highest = jnp.max(peak[head], axis=1, keepdims=True)
            peak[head] = jnp.broadcast_to(highest, (BLOCK, BLOCK))
            if first:
                peaks[block, head] = peak[head]
            else:
                factor = jnp.exp2((peaks[block, head] - peak[head]) * EXPONENT)
                totals[block, head] = totals_in[block, head] * factor
                sums[block, head] = sums_in[block, head] * factor
        over_blocks(weigh)

        if not first:
            for head in range(heads):
                norm = jnp.sum(totals[block, head], axis=1, keepdims=True)
                out_ref[:, head * HDIM : (head + 1) * HDIM] = (sums[block, head] / norm).astype(
                    jnp.bfloat16
                )

    if not first:
        loads[0].wait()
        partial_ref[...] = jnp.dot(
            out_ref[...], weight[...], preferred_element_type=jnp.float32
        ).astype(jnp.bfloat16)


def attention_part(first, chosen_rows, swaps, count, place, storm_mask, query, state, parts, *projection):
    rows, width = query.shape
    heads = width // HDIM
    blocks = count * (rows // BLOCK)
    vmem = pl.BlockSpec(memory_space=pltpu.VMEM)
    hbm = pl.BlockSpec(memory_space=pl.ANY)
    running = (rows // BLOCK, heads, BLOCK, BLOCK)
    taken = jax.ShapeDtypeStruct((rows, width), jnp.bfloat16)
    scratch = [
        pltpu.VMEM((count, rows, 2 * HDIM), jnp.bfloat16),
        pltpu.VMEM((heads, BLOCK, BLOCK), jnp.float32),
        pltpu.VMEM((blocks, heads, BLOCK, BLOCK), jnp.float32),
    ]
    if first:
        specs = [hbm, hbm] + [vmem] * len(parts)
        out_shape = [taken] + [jax.ShapeDtypeStruct(running, jnp.float32)] * 3
    else:
        weight, column, columns = projection
        place = jnp.stack([place, column // columns])
        parts = [*parts, weight]
        specs = [vmem] * (3 + len(parts)) + [hbm]
        out_shape = [
            jax.ShapeDtypeStruct((BLOCK, wide), jnp.bfloat16) for wide in (width, columns)
        ]
        scratch += [pltpu.VMEM(running, jnp.float32)] * 2
        scratch += [pltpu.VMEM((weight.shape[0], columns), jnp.bfloat16)]
    scratch += [pltpu.SMEM((blocks + 1,), jnp.int32)]
    scratch += [pltpu.SemaphoreType.DMA((2,)) if first else pltpu.SemaphoreType.DMA]
    return pl.pallas_call(
        functools.partial(attention_kernel, len(parts) - len(projection[:1]), swaps, first, chosen_rows),
        grid_spec=pltpu.PrefetchScalarGridSpec(
            num_scalar_prefetch=2,
            grid=(1,),
            in_specs=specs,
            out_specs=[vmem] * len(out_shape),
            scratch_shapes=scratch,
        ),
        out_shape=out_shape,
        compiler_params=pltpu.CompilerParams(vmem_limit_bytes=VMEM_LIMIT),
        name="attend_first" if first else "attend_rest",
    )(place.astype(jnp.int32).reshape(-1), storm_mask, query, *state, *parts)


def attend(queries, packed, place, devices, storm_mask, *projection):
    every = tuple(range(queries.shape[0] // BLOCK))
    if devices != 8:
        everyone = lax.all_gather(packed, "ctx", axis=0, tiled=False)
        state = attention_part(
            True, every, (), devices, place, storm_mask, queries, [packed], [everyone]
        )
        query, *state = state
        nothing = jnp.zeros_like(storm_mask)
        swaps, parts, storm_mask = (), [everyone[:1]], nothing
    else:

        def swap(array, bits):
            return lax.ppermute(array, "ctx", [(i, i ^ bits) for i in range(devices)])

        near = [swap(packed[None], bits) for bits in (6, 2, 4)]
        query, *state = attention_part(
            True, every, (0, 1), 2, place, storm_mask, queries, [packed], [swap(packed[None], 1)]
        )
        swaps, parts = (6, 2, 4, 7, 3, 5), near + [swap(array, 1) for array in near]
    attended, partials = [], []
    for block in every:
        if partials:
            query = after(query, partials[-1])
        rows, partial = attention_part(
            False, (block,), swaps, len(swaps) or 1, place, storm_mask, query, state, parts, *projection
        )
        attended.append(rows)
        partials.append(partial)
    return attended, partials


def project_kernel(first_ref, *refs):
    *attended_refs, weight_ref, out_ref = refs
    at = 0
    for ref in attended_refs:
        rows = ref.shape[0]
        out_ref[at : at + rows] = jnp.dot(
            ref[...], weight_ref[...], preferred_element_type=jnp.float32
        ).astype(jnp.bfloat16)
        at += rows


def project(attended, out_weight, first, columns):
    depth = out_weight.shape[0]
    rows = sum(array.shape[0] for array in attended)
    tile = min(TILE, columns)
    return pl.pallas_call(
        project_kernel,
        grid_spec=pltpu.PrefetchScalarGridSpec(
            num_scalar_prefetch=1,
            grid=(columns // tile,),
            in_specs=[pl.BlockSpec(array.shape, lambda i, first: (0, 0)) for array in attended]
            + [pl.BlockSpec((depth, tile), lambda i, first: (0, first[0] + i))],
            out_specs=pl.BlockSpec((rows, tile), lambda i, first: (0, i)),
        ),
        out_shape=jax.ShapeDtypeStruct((rows, columns), jnp.bfloat16),
        compiler_params=pltpu.CompilerParams(vmem_limit_bytes=VMEM_LIMIT),
        name="project",
    )((first // tile).astype(jnp.int32).reshape(1), *attended, out_weight)


def after(array, *earlier):
    return lax.optimization_barrier((array, *earlier))[0]


def added(*arrays):
    wide = [array.astype(jnp.float32) for array in arrays]
    return functools.reduce(lambda a, b: a + b, wide).astype(jnp.bfloat16)


def line_sum(attend_now, out_weight):
    place = lax.axis_index("tp")
    quarter = out_weight.shape[1] // 4
    upper = place >= 2
    far_outer = jnp.where(upper, 0, 3) * quarter
    far_inner = jnp.where(upper, 1, 2) * quarter
    near = jnp.where(upper, 5 - place, 1 - place) * quarter
    own = place * quarter
    half = quarter // 2
    fourth = quarter // 4
    halves = ((0, half), (half, half))
    attended, partials = attend_now(far_outer, half)
    projected, chain = [partials[-1]], []
    ahead = partials[0].shape[0]

    def part(first, columns):
        source = [after(attended[0], projected[-1]), *attended[1:]]
        projected.append(project(source, out_weight, first, columns))
        return projected[-1]

    def step(*arrays):
        first = after(arrays[0], chain[-1]) if chain else arrays[0]
        chain.append(added(first, *arrays[1:]))
        return chain[-1]

    def inward(array):
        return lax.ppermute(array, "tp", [(0, 1), (3, 2)])

    def across(array):
        return lax.ppermute(array, "tp", [(1, 2), (2, 1)])

    def outward(array):
        return lax.ppermute(array, "tp", [(1, 0), (2, 3)])

    outer_parts = [*partials, part(far_outer + half, half)]
    outer_sums = [inward(array) for array in outer_parts]
    inner_parts = [part(far_inner + at, size) for at, size in halves]
    inner_sums = [inward(array) for array in inner_parts]
    to_outer, to_own, returned, direct = [None] * 3, [None] * 2, [None] * 3, [None] * 2

    def send_outer(at):
        to_outer[at] = across(step(outer_parts[at], outer_sums[at]))

    def send_inner(at):
        to_own[at] = across(step(inner_parts[at], inner_sums[at]))
        direct[at] = inward(after(near_parts[at], chain[-1]))

    def send_back(at):
        returned[at] = outward(step(near_pieces[at], to_outer[at]))

    send_outer(0)
    send_outer(1)
    projected.append(chain[-1])
    near_parts = [part(near + at, size) for at, size in halves]
    near_pieces = [near_parts[0][:ahead], near_parts[0][ahead:], near_parts[1]]
    send_outer(2)
    send_inner(0)
    send_back(0)
    send_back(1)
    mine = part(own, quarter)
    left = step(mine[:, :half], jnp.concatenate(returned[:2], axis=0))
    send_inner(1)
    send_back(2)
    left = step(left, to_own[0], direct[0])
    right = step(mine[:, half:], returned[2], to_own[1], direct[1])
    return jnp.concatenate([left, right], axis=1)


def body(mesh, queries, keys, values, out_weight, storm_mask):
    place = lax.axis_index("ctx")
    heads = queries.shape[1] // HDIM
    shared_head = lax.axis_index("tp") * heads // GQ
    packed = pack_head(keys, values, shared_head)

    def attend_now(first, columns):
        return attend(
            queries, packed, place, mesh.shape["ctx"], storm_mask, out_weight, first, columns
        )

    if mesh.shape["tp"] == 4:
        return line_sum(attend_now, out_weight)
    _, partials = attend_now(jnp.int32(0), out_weight.shape[1])
    partial = jnp.concatenate(partials, axis=0)
    return lax.psum_scatter(partial, "tp", scatter_dimension=1, tiled=True)


def solution(mesh):
    placed = (P("ctx", "tp"), P("ctx", None), P("ctx", None), P("tp", None), P())
    return jax.shard_map(
        functools.partial(body, mesh),
        mesh=mesh,
        in_specs=placed,
        out_specs=P("ctx", "tp"),
        check_vma=False,
    )
```
